32 devices in a mesh: groups: 2 (over y), row: 4 (over z), col: 4 (over x, core).
Axes of the slice: x: 2, y: 2, z: 4, core: 2. Of those that a mesh axis runs over, the one named last changes fastest.
Arguments:
- grad_users: bfloat16 [32768, 128], P(('groups', 'row', 'col')), parts along dimension 0, may hold values from -6 to 6
- grad_items: bfloat16 [16384, 128], P(('groups', 'col', 'row')), parts along dimension 0, may hold values from -6 to 6
- user_degree: int32 [32768], P(('groups', 'row', 'col')), parts along dimension 0, may hold values from 1 to 4
- item_degree: int32 [16384], P(('groups', 'col', 'row')), parts along dimension 0, may hold values from 1 to 4
- tile_values: bfloat16 [768, 256, 256], P(('groups', 'row', 'col')), parts along dimension 0, may hold values from -0.109375 to 0.109375
- tile_row: int32 [768], P(('groups', 'row', 'col')), parts along dimension 0, may hold values from 0 to 15, as said below
- tile_col: int32 [768], P(('groups', 'row', 'col')), parts along dimension 0, may hold values from 0 to 7, as said below
Outputs:
- user_grad: bfloat16 [32768, 128], P(('groups', 'row', 'col')), parts along dimension 0
- item_grad: bfloat16 [16384, 128], P(('groups', 'col', 'row')), parts along dimension 0
The draws below stay inside these ranges and needn't reach their ends.
There are 2 independent parts, one for each index of `groups`. The reference program is written for one: setup_inputs(seed, part) draws one part's arguments, and reference() takes and returns one part's arrays. A program takes and returns all parts, laid end to end along the dimension named above; each array names one. Nothing has to cross between parts.
Inputs may be any that keep to these rules, and one draw needn't show every extreme that they name: tile_row counts user blocks inside the row range of the owning device (slot s // 24 = r * 4 + c owns row range r); the 24 tiles of one owner stand at distinct (tile_row, tile_col) positions. tile_col counts item blocks inside the column range c of the owning device.
All inputs are finite; a program needn't handle non-finite values.
Results may differ from the reference program's by a relative error of at most 0.0075.
Values may be sent and summed in bfloat16 or wider, within the bound.
A program may use at most 64 MiB of HBM per device.

```python
import jax
import jax.numpy as jnp
from jax import lax

D = 128
TILE = 256
LAYERS = 2
USER_BLOCKS_PER = 16
I_BLK_DEV = 8
TILE_DEV = 24
USERS = 16384
ITEMS = 8192
TILES = 384
N_ROW = 4
N_COL = 4


def slot_positions(key):
    owner_keys = jax.random.split(key, N_ROW * N_COL)

    def one_owner(owner_key):
        return jax.random.permutation(owner_key, jnp.arange(USER_BLOCKS_PER * I_BLK_DEV, dtype=jnp.int32))[:TILE_DEV]
    return jax.vmap(one_owner)(owner_keys).reshape(-1).astype(jnp.int32)


def draw_tile_row(key, part):
    slots = slot_positions(key)
    return (slots // I_BLK_DEV).astype(jnp.int32)


def draw_tile_col(key, part):
    slots = slot_positions(key)
    return (slots % I_BLK_DEV).astype(jnp.int32)


def with_ends(values, key, least, largest):
    dims = values.shape
    index_at = [jax.random.randint(jax.random.fold_in(key, axis), (), 0, dims[axis]) for axis in range(len(dims))]
    values = values.at[tuple(index_at)].set(least)
    longest = dims.index(max(dims))
    index_at[longest] = (index_at[longest] + 1) % dims[longest]
    return values.at[tuple(index_at)].set(largest)


def steps_of(own_key, extent, cuts, smallest, top_value):
    level, own = 1.0, jax.random.fold_in(own_key, 6)
    for position, blocks in cuts:
        steps = jnp.exp(jax.random.uniform(jax.random.fold_in(own, position), (blocks,), jnp.float32, smallest / len(cuts), top_value / len(cuts)))
        level = level * jnp.repeat(steps, extent[position] // blocks).reshape([-1 if axis == position else 1 for axis in range(len(extent))])
    return level


def centred(key, dims, deviation, most, shards=(), kind=jnp.bfloat16):
    result = jax.random.normal(key, dims, jnp.float32) * deviation
    if len(shards) > 0:
        result = steps_of(key, dims, shards, -0.22, 0.18) * result
    return jnp.clip(result, min=-most, max=most).astype(kind)


def setup_inputs(seed: int = 0, part: int = 0) -> dict:
    seeds = jax.random.split(jax.random.key(seed), 8)
    own_keys = jax.random.split(jax.random.fold_in(seeds[7], part), 8)
    return {
        "grad_users": centred(own_keys[0], (USERS, D), 1.0, 6.0, ((0, 16),)),
        "grad_items": centred(own_keys[1], (ITEMS, D), 1.0, 6.0, ((0, 16),)),
        "user_degree": with_ends(jax.random.randint(own_keys[2], (USERS,), 1, 5), jax.random.fold_in(own_keys[2], 1), 1, 4).astype(jnp.int32),
        "item_degree": with_ends(jax.random.randint(own_keys[3], (ITEMS,), 1, 5), jax.random.fold_in(own_keys[3], 1), 1, 4).astype(jnp.int32),
        "tile_values": centred(own_keys[4], (TILES, TILE, TILE), (TILE * TILE_DEV * N_ROW // I_BLK_DEV) ** -0.5, 0.109375, ((0, 16),)),
        "tile_row": draw_tile_row(jax.random.fold_in(jax.random.fold_in(seeds[7], part), 71), part),
        "tile_col": draw_tile_col(jax.random.fold_in(jax.random.fold_in(seeds[7], part), 71), part),
    }


def reference(grad_users, grad_items, user_degree, item_degree, tile_values, tile_row, tile_col):
    weight_per_layer = 1.0 / (LAYERS + 1)
    user_scale = lax.rsqrt(user_degree.astype(jnp.float32))[:, None]
    item_scale = lax.rsqrt(item_degree.astype(jnp.float32))[:, None]
    user_base = weight_per_layer * grad_users.astype(jnp.float32)
    item_base = weight_per_layer * grad_items.astype(jnp.float32)
    users_now = user_base.astype(jnp.bfloat16)
    items_now = item_base.astype(jnp.bfloat16)
    tiles = tile_values.reshape(N_ROW, N_COL, TILE_DEV, TILE, TILE)
    row_index = tile_row.reshape(N_ROW, N_COL, TILE_DEV).astype(jnp.int32)
    col_index = tile_col.reshape(N_ROW, N_COL, TILE_DEV).astype(jnp.int32)
    col_range = jnp.arange(N_COL, dtype=jnp.int32)[:, None]
    for layer_position in range(LAYERS):
        scaled_items = (item_scale * items_now.astype(jnp.float32)).astype(jnp.bfloat16).reshape(N_COL, I_BLK_DEV, TILE, D)
        scaled_users = (user_scale * users_now.astype(jnp.float32)).astype(jnp.bfloat16).reshape(N_ROW, USER_BLOCKS_PER, TILE, D)

        def one_range(carry, inputs):
            block_tiles, block_rows, block_cols, users_block = inputs
            tiles_wide = block_tiles.astype(jnp.float32)
            picked = scaled_items[col_range, block_cols].astype(jnp.float32)
            matrix_product = jnp.einsum('ctab,ctbd->ctad', tiles_wide, picked)
            partial_value = jnp.zeros((N_COL, USER_BLOCKS_PER, TILE, D), jnp.float32).at[col_range, block_rows].add(matrix_product)
            rounded_values = lax.optimization_barrier(partial_value.astype(jnp.bfloat16))
            user_sum = lax.optimization_barrier(jnp.sum(rounded_values.astype(jnp.float32), axis=0))
            picked_users = users_block[block_rows].astype(jnp.float32)
            product_items = jnp.einsum('ctba,ctbd->ctad', tiles_wide, picked_users)
            carry = carry.at[col_range, block_cols].add(product_items)
            return (carry, user_sum)
        start = jnp.zeros((N_COL, I_BLK_DEV, TILE, D), jnp.float32)
        item_sums, user_partial_sums = lax.scan(one_range, start, (tiles, row_index, col_index, scaled_users))
        users_now = (user_base + user_scale * user_partial_sums.reshape(USERS, D)).astype(jnp.bfloat16)
        items_now = (item_base + item_scale * item_sums.reshape(ITEMS, D)).astype(jnp.bfloat16)
    return (users_now, items_now)
```

```python
import functools

import jax
import jax.numpy as jnp
from jax import lax
from jax.experimental import pallas as pl
from jax.experimental.pallas import tpu as pltpu
from jax.sharding import PartitionSpec as P

LAYERS = 2
MESH = pl.DeviceIdType.MESH
WEIGHT = 1.0 / (LAYERS + 1)


def kernel(
    n_row, n_col, n_tiles, tile, width, u_rows, i_rows,
    idx, gu, gi, su, si, tiles_hbm,
    out_u, out_i,
    users_0, users_1, items_0, items_1, up_out, up_in, ip_out, ip_in, sum_u, sum_i, tiles, tiles_t,
    u_send, u_recv, i_send, i_recv, tile_sem,
):
    mr, mc = lax.axis_index("row"), lax.axis_index("col")
    u_blocks = u_rows * n_col // tile
    i_blocks = i_rows * n_row // tile
    at_row, at_col = 0, n_tiles
    at_prev_row, at_prev_col = 2 * n_tiles, 3 * n_tiles
    at_last_row, at_last_col = 4 * n_tiles, 4 * n_tiles + u_blocks

    barrier = pltpu.get_barrier_semaphore()

    def greet(axis, me, n):
        def body(d, carry):
            pl.semaphore_signal(
                barrier, inc=1, device_id={axis: lax.rem(me + d, n)}, device_id_type=MESH
            )
            return carry

        lax.fori_loop(1, n, body, 0)

    greet("row", mr, n_row)
    greet("col", mc, n_col)
    tile_copy = pltpu.make_async_copy(tiles_hbm, tiles, tile_sem)
    tile_copy.start()

    users_all, items_all = (users_0, users_1), (items_0, items_1)

    def part(ref, p, rows):
        if rows % tile == 0:
            k = rows // tile
            return ref.at[pl.ds(p * k, k)]
        per = tile // rows
        return ref.at[lax.div(p, per), pl.ds(pl.multiple_of(lax.rem(p, per) * rows, rows), rows)]

    def slot(ref, l, d, rows):
        return ref.at[l, d] if rows % tile == 0 else ref.at[l, d, 0]

    def gather_items(l, d):
        return pltpu.make_async_remote_copy(
            src_ref=part(items_all[l], mr, i_rows),
            dst_ref=part(items_all[l], mr, i_rows),
            send_sem=i_send.at[l, 0, d],
            recv_sem=i_recv.at[l, 0, d],
            device_id={"row": lax.rem(mr + d, n_row)},
            device_id_type=MESH,
        )

    def gather_users(l, d):
        return pltpu.make_async_remote_copy(
            src_ref=part(users_all[l], mc, u_rows),
            dst_ref=part(users_all[l], mc, u_rows),
            send_sem=u_send.at[l, 0, d],
            recv_sem=u_recv.at[l, 0, d],
            device_id={"col": lax.rem(mc + d, n_col)},
            device_id_type=MESH,
        )

    def scatter_items(l, d):
        peer = lax.rem(mr + d, n_row)
        return pltpu.make_async_remote_copy(
            src_ref=part(ip_out.at[l], peer, i_rows),
            dst_ref=slot(ip_in, l, d, i_rows),
            send_sem=i_send.at[l, 1, d],
            recv_sem=i_recv.at[l, 1, d],
            device_id={"row": peer},
            device_id_type=MESH,
        )

    def scatter_users(l, d):
        peer = lax.rem(mc + d, n_col)
        return pltpu.make_async_remote_copy(
            src_ref=part(up_out.at[l], peer, u_rows),
            dst_ref=slot(up_in, l, d, u_rows),
            send_sem=u_send.at[l, 1, d],
            recv_sem=u_recv.at[l, 1, d],
            device_id={"col": peer},
            device_id_type=MESH,
        )

    def each(copies, l, n, act):
        def body(d, carry):
            act(copies(l, d))
            return carry

        lax.fori_loop(1, n, body, 0)

    start = lambda c: c.start()
    wait_recv = lambda c: c.wait_recv()
    wait_send = lambda c: c.wait_send()

    def begin(rows, own, grad, scale, gathered):
        chunk = min(rows, 128)

        def body(k, carry):
            here = pl.ds(pl.multiple_of(k * chunk, chunk), chunk)
            now = (WEIGHT * grad[here, :].astype(jnp.float32)).astype(jnp.bfloat16)
            at = own + k * chunk
            mine = pl.ds(pl.multiple_of(lax.rem(at, tile), chunk), chunk)
            gathered[0][lax.div(at, tile), mine, :] = (
                scale[here, :] * now.astype(jnp.float32)
            ).astype(jnp.bfloat16)
            return carry

        lax.fori_loop(0, rows // chunk, body, 0)

    begin(i_rows, mr * i_rows, gi, si, items_all)
    begin(u_rows, mc * u_rows, gu, su, users_all)
    pl.semaphore_wait(barrier, n_row + n_col - 2)
    each(gather_items, 0, n_row, start)
    each(gather_users, 0, n_col, start)

    sum_u[0] = jnp.zeros((tile, width), jnp.float32)
    sum_i[0] = jnp.zeros((tile, width), jnp.float32)
    tile_copy.wait()

    def turn(n, carry):
        tiles_t[n] = tiles[n].T
        return carry

    lax.fori_loop(0, n_tiles, turn, 0)

    group = 4 if n_tiles % 4 == 0 else 1

    def products(l, mats, blocks, sums, at_block, at_prev):
        def body(g, carry):
            parts = []
            for k in range(group):
                n = g * group + k
                b = idx[at_block + n]
                parts.append(jnp.dot(mats[n], blocks[l][b], preferred_element_type=jnp.float32))
            for k in range(group):
                n = g * group + k
                sums[n + 1] = parts[k] + sums[idx[at_prev + n]]
            return carry

        lax.fori_loop(0, n_tiles // group, body, 0)

    def stage(l, out, sums, at_last, blocks):
        def body(b, carry):
            out[l, b] = sums[idx[at_last + b]].astype(jnp.bfloat16)
            return carry

        lax.fori_loop(0, blocks, body, 0)

    def update(l, n, rows, own, grad, scale, out, inn, result, gathered):
        chunk = min(rows, 128)

        def body(k, carry):
            here = pl.ds(pl.multiple_of(k * chunk, chunk), chunk)
            at = own + k * chunk
            block = lax.div(at, tile)
            mine = pl.ds(pl.multiple_of(lax.rem(at, tile), chunk), chunk)
            total = out[l, block, mine, :].astype(jnp.float32)
            sub = min(rows, tile)
            sub_at = pl.ds(pl.multiple_of(lax.rem(k * chunk, sub), chunk), chunk)

            def add(d, total):
                return total + inn[l, d, lax.div(k * chunk, sub), sub_at, :].astype(jnp.float32)

            if n <= 8:
                for d in range(1, n):
                    total = add(d, total)
            else:
                total = lax.fori_loop(1, n, add, total)
            factor = scale[here, :]
            now = (WEIGHT * grad[here, :].astype(jnp.float32) + factor * total).astype(jnp.bfloat16)
            if l + 1 < LAYERS:
                gathered[l + 1][block, mine, :] = (factor * now.astype(jnp.float32)).astype(jnp.bfloat16)
            else:
                result[here, :] = now
            return carry

        lax.fori_loop(0, rows // chunk, body, 0)

    for l in range(LAYERS):
        each(gather_users, l, n_col, wait_recv)
        products(l, tiles_t, users_all, sum_i, at_row, at_prev_col)
        stage(l, ip_out, sum_i, at_last_col, i_blocks)
        each(scatter_items, l, n_row, start)
        each(gather_items, l, n_row, wait_recv)
        products(l, tiles, items_all, sum_u, at_col, at_prev_row)
        stage(l, up_out, sum_u, at_last_row, u_blocks)
        each(scatter_users, l, n_col, start)
        each(scatter_items, l, n_row, wait_recv)
        update(l, n_row, i_rows, mr * i_rows, gi, si, ip_out, ip_in, out_i, items_all)
        if l + 1 < LAYERS:
            each(gather_items, l + 1, n_row, start)
        each(scatter_users, l, n_col, wait_recv)
        update(l, n_col, u_rows, mc * u_rows, gu, su, up_out, up_in, out_u, users_all)
        if l + 1 < LAYERS:
            each(gather_users, l + 1, n_col, start)
    for l in range(LAYERS):
        each(gather_items, l, n_row, wait_send)
        each(gather_users, l, n_col, wait_send)
        each(scatter_items, l, n_row, wait_send)
        each(scatter_users, l, n_col, wait_send)


def shards(grad_users, grad_items, user_degree, item_degree, tile_values, tile_row, tile_col):
    n_row, n_col = lax.axis_size("row"), lax.axis_size("col")
    n_tiles, tile = tile_values.shape[:2]
    u_rows, width = grad_users.shape
    i_rows = grad_items.shape[0]
    u_blocks, i_blocks = u_rows * n_col // tile, i_rows * n_row // tile
    su = jnp.broadcast_to(lax.rsqrt(user_degree.astype(jnp.float32))[:, None], (u_rows, width))
    si = jnp.broadcast_to(lax.rsqrt(item_degree.astype(jnp.float32))[:, None], (i_rows, width))
    slot = jnp.arange(n_tiles, dtype=jnp.int32)

    def latest(keys, wanted, before):
        hit = (keys[None, :] == wanted[:, None]) & (slot[None, :] < before[:, None])
        return jnp.max(jnp.where(hit, slot[None, :] + 1, 0), axis=1)

    idx = jnp.concatenate(
        [
            tile_row,
            tile_col,
            latest(tile_row, tile_row, slot),
            latest(tile_col, tile_col, slot),
            latest(tile_row, jnp.arange(u_blocks, dtype=jnp.int32), jnp.full(u_blocks, n_tiles)),
            latest(tile_col, jnp.arange(i_blocks, dtype=jnp.int32), jnp.full(i_blocks, n_tiles)),
        ]
    )
    u_sub, i_sub = min(u_rows, tile), min(i_rows, tile)
    vmem = pl.BlockSpec(memory_space=pltpu.VMEM)
    bf16, f32 = jnp.bfloat16, jnp.float32
    return pl.pallas_call(
        functools.partial(kernel, n_row, n_col, n_tiles, tile, width, u_rows, i_rows),
        out_shape=(
            jax.ShapeDtypeStruct((u_rows, width), bf16),
            jax.ShapeDtypeStruct((i_rows, width), bf16),
        ),
        in_specs=[pl.BlockSpec(memory_space=pltpu.SMEM), vmem, vmem, vmem, vmem,
                  pl.BlockSpec(memory_space=pl.ANY)],
        out_specs=(vmem, vmem),
        scratch_shapes=[
            pltpu.VMEM((u_blocks, tile, width), bf16),
            pltpu.VMEM((u_blocks, tile, width), bf16),
            pltpu.VMEM((i_blocks, tile, width), bf16),
            pltpu.VMEM((i_blocks, tile, width), bf16),
            pltpu.VMEM((LAYERS, u_blocks, tile, width), bf16),
            pltpu.VMEM((LAYERS, n_col, u_rows // u_sub, u_sub, width), bf16),
            pltpu.VMEM((LAYERS, i_blocks, tile, width), bf16),
            pltpu.VMEM((LAYERS, n_row, i_rows // i_sub, i_sub, width), bf16),
            pltpu.VMEM((n_tiles + 1, tile, width), f32),
            pltpu.VMEM((n_tiles + 1, tile, width), f32),
            pltpu.VMEM((n_tiles, tile, tile), bf16),
            pltpu.VMEM((n_tiles, tile, tile), bf16),
            pltpu.SemaphoreType.DMA((LAYERS, 2, n_col)),
            pltpu.SemaphoreType.DMA((LAYERS, 2, n_col)),
            pltpu.SemaphoreType.DMA((LAYERS, 2, n_row)),
            pltpu.SemaphoreType.DMA((LAYERS, 2, n_row)),
            pltpu.SemaphoreType.DMA,
        ],
        compiler_params=pltpu.CompilerParams(
            collective_id=0, has_side_effects=True, vmem_limit_bytes=40 * 1024 * 1024
        ),
    )(idx, grad_users, grad_items, su, si, tile_values)


def solution(mesh):
    return jax.shard_map(
        shards,
        mesh=mesh,
        in_specs=(
            P(("groups", "row", "col"), None),
            P(("groups", "col", "row"), None),
            P(("groups", "row", "col")),
            P(("groups", "col", "row")),
            P(("groups", "row", "col"), None, None),
            P(("groups", "row", "col")),
            P(("groups", "row", "col")),
        ),
        out_specs=(P(("groups", "row", "col"), None), P(("groups", "col", "row"), None)),
        check_vma=False,
    )
```

```python
import functools

import jax
import jax.numpy as jnp
from jax import lax
from jax.experimental import pallas as pl
from jax.experimental.pallas import tpu as pltpu
from jax.sharding import PartitionSpec as P

LAYERS = 2
MESH = pl.DeviceIdType.MESH
WEIGHT = 1.0 / (LAYERS + 1)


def kernel(
    n_row, n_col, n_tiles, tile, width, u_rows, i_rows,
    idx, gu, gi, su, si, tiles_hbm,
    out_u, out_i,
    users_0, users_1, items_0, items_1, up_out, up_in, ip_out, ip_in, sum_u, sum_i, tiles, tiles_t,
    u_send, u_recv, i_send, i_recv, tile_sem,
):
    mr, mc = lax.axis_index("row"), lax.axis_index("col")
    u_blocks = u_rows * n_col // tile
    i_blocks = i_rows * n_row // tile
    at_row, at_col = 0, n_tiles
    at_prev_row, at_prev_col = 2 * n_tiles, 3 * n_tiles
    at_last_row, at_last_col = 4 * n_tiles, 4 * n_tiles + u_blocks

    barrier = pltpu.get_barrier_semaphore()

    def greet(axis, me, n):
        def body(d, carry):
            pl.semaphore_signal(
                barrier, inc=1, device_id={axis: lax.rem(me + d, n)}, device_id_type=MESH
            )
            return carry

        lax.fori_loop(1, n, body, 0)

    greet("row", mr, n_row)
    greet("col", mc, n_col)
    tile_copy = pltpu.make_async_copy(tiles_hbm, tiles, tile_sem)
    tile_copy.start()

    users_all, items_all = (users_0, users_1), (items_0, items_1)

    def part(ref, p, rows):
        if rows % tile == 0:
            k = rows // tile
            return ref.at[pl.ds(p * k, k)]
        per = tile // rows
        return ref.at[lax.div(p, per), pl.ds(pl.multiple_of(lax.rem(p, per) * rows, rows), rows)]

    def slot(ref, l, d, rows):
        return ref.at[l, d] if rows % tile == 0 else ref.at[l, d, 0]

    def address(at, rows, chunk):
        sub = min(rows, tile)
        return lax.div(at, sub), pl.ds(pl.multiple_of(lax.rem(at, sub), chunk), chunk)

    class Route:
        def __init__(self, axis, me, n, rows, gathered, out, inn, send, recv):
            self.n, self.rows, self.me, self.axis = n, rows, me, axis
            self.gathered, self.out, self.inn, self.send, self.recv = gathered, out, inn, send, recv
            self.relayed = n == 4
            one = me + 1 - 2 * lax.rem(me, 2)
            self.peer = (me, one, lax.rem(me + 2, 4), lax.rem(one + 2, 4))
            self.terms = 3 if self.relayed else n

        def remote(self, src, dst, l, kind, d, peer):
            return pltpu.make_async_remote_copy(
                src_ref=src,
                dst_ref=dst,
                send_sem=self.send.at[l, kind, d],
                recv_sem=self.recv.at[l, kind, d],
                device_id={self.axis: peer},
                device_id_type=MESH,
            )

        def gather(self, l, d):
            if self.relayed:
                owner, to = self.peer[2 if d == 3 else 0], self.peer[2 if d == 2 else 1]
            else:
                owner, to = self.me, lax.rem(self.me + d, self.n)
            at = part(self.gathered[l], owner, self.rows)
            return self.remote(at, at, l, 0, d, to)

        def scatter(self, l, d):
            if self.relayed:
                piece, to = self.peer[d], self.peer[2 if d == 2 else 1]
            else:
                piece = to = lax.rem(self.me + d, self.n)
            return self.remote(
                part(self.out.at[l], piece, self.rows), slot(self.inn, l, d, self.rows), l, 1, d, to
            )

        def each(self, copies, l, act, some):
            if self.relayed:
                for d in some:
                    act(copies(l, d))
            else:
                def body(d, carry):
                    act(copies(l, d))
                    return carry

                lax.fori_loop(1, self.n, body, 0)

        def gather_start(self, l):
            self.each(self.gather, l, lambda c: c.start(), (2, 1))

        def gather_relay(self, l):
            if self.relayed:
                self.gather(l, 2).wait_recv()
                self.gather(l, 3).start()

        def gather_wait(self, l):
            self.each(self.gather, l, lambda c: c.wait_recv(), (1, 3))

        def scatter_start(self, l):
            self.each(self.scatter, l, lambda c: c.start(), (3, 1))

        def scatter_relay(self, l):
            if self.relayed:
                self.scatter(l, 3).wait_recv()
                chunk = min(self.rows, 128)

                def body(k, carry):
                    at = self.peer[2] * self.rows + k * chunk
                    block = lax.div(at, tile)
                    mine = pl.ds(pl.multiple_of(lax.rem(at, tile), chunk), chunk)
                    sub, there = address(k * chunk, self.rows, chunk)
                    self.out[l, block, mine, :] = (
                        self.out[l, block, mine, :].astype(jnp.float32)
                        + self.inn[l, 3, sub, there, :].astype(jnp.float32)
                    ).astype(jnp.bfloat16)
                    return carry

                lax.fori_loop(0, self.rows // chunk, body, 0)
                self.scatter(l, 2).start()

        def scatter_wait(self, l):
            self.each(self.scatter, l, lambda c: c.wait_recv(), (1, 2))

        def finish(self, l):
            self.each(self.gather, l, lambda c: c.wait_send(), (1, 2, 3))
            self.each(self.scatter, l, lambda c: c.wait_send(), (1, 2, 3))

    items = Route("row", mr, n_row, i_rows, items_all, ip_out, ip_in, i_send, i_recv)
    users = Route("col", mc, n_col, u_rows, users_all, up_out, up_in, u_send, u_recv)

    def begin(rows, own, grad, scale, gathered):
        chunk = min(rows, 128)

        def body(k, carry):
            here = pl.ds(pl.multiple_of(k * chunk, chunk), chunk)
            now = (WEIGHT * grad[here, :].astype(jnp.float32)).astype(jnp.bfloat16)
            at = own + k * chunk
            mine = pl.ds(pl.multiple_of(lax.rem(at, tile), chunk), chunk)
            gathered[0][lax.div(at, tile), mine, :] = (
                scale[here, :] * now.astype(jnp.float32)
            ).astype(jnp.bfloat16)
            return carry

        lax.fori_loop(0, rows // chunk, body, 0)

    begin(i_rows, mr * i_rows, gi, si, items_all)
    begin(u_rows, mc * u_rows, gu, su, users_all)
    pl.semaphore_wait(barrier, n_row + n_col - 2)
    items.gather_start(0)
    users.gather_start(0)

    sum_u[0] = jnp.zeros((tile, width), jnp.float32)
    sum_i[0] = jnp.zeros((tile, width), jnp.float32)
    tile_copy.wait()

    def turn(n, carry):
        tiles_t[n] = tiles[n].T
        return carry

    lax.fori_loop(0, n_tiles, turn, 0)

    group = 4 if n_tiles % 4 == 0 else 1

    def products(l, mats, blocks, sums, at_block, at_prev):
        def body(g, carry):
            parts = []
            for k in range(group):
                n = g * group + k
                b = idx[at_block + n]
                parts.append(jnp.dot(mats[n], blocks[l][b], preferred_element_type=jnp.float32))
            for k in range(group):
                n = g * group + k
                sums[n + 1] = parts[k] + sums[idx[at_prev + n]]
            return carry

        lax.fori_loop(0, n_tiles // group, body, 0)

    def stage(l, out, sums, at_last, blocks):
        def body(b, carry):
            out[l, b] = sums[idx[at_last + b]].astype(jnp.bfloat16)
            return carry

        lax.fori_loop(0, blocks, body, 0)

    def update(l, n, rows, own, grad, scale, out, inn, result, gathered):
        chunk = min(rows, 128)

        def body(k, carry):
            here = pl.ds(pl.multiple_of(k * chunk, chunk), chunk)
            at = own + k * chunk
            block = lax.div(at, tile)
            mine = pl.ds(pl.multiple_of(lax.rem(at, tile), chunk), chunk)
            total = out[l, block, mine, :].astype(jnp.float32)
            sub, there = address(k * chunk, rows, chunk)

            def add(d, total):
                return total + inn[l, d, sub, there, :].astype(jnp.float32)

            if n <= 8:
                for d in range(1, n):
                    total = add(d, total)
            else:
                total = lax.fori_loop(1, n, add, total)
            factor = scale[here, :]
            now = (WEIGHT * grad[here, :].astype(jnp.float32) + factor * total).astype(jnp.bfloat16)
            if l + 1 < LAYERS:
                gathered[l + 1][block, mine, :] = (factor * now.astype(jnp.float32)).astype(jnp.bfloat16)
            else:
                result[here, :] = now
            return carry

        lax.fori_loop(0, rows // chunk, body, 0)

    for l in range(LAYERS):
        users.gather_relay(l)
        items.gather_relay(l)
        users.gather_wait(l)
        products(l, tiles_t, users_all, sum_i, at_row, at_prev_col)
        stage(l, ip_out, sum_i, at_last_col, i_blocks)
        items.scatter_start(l)
        items.gather_wait(l)
        products(l, tiles, items_all, sum_u, at_col, at_prev_row)
        stage(l, up_out, sum_u, at_last_row, u_blocks)
        users.scatter_start(l)
        items.scatter_relay(l)
        users.scatter_relay(l)
        items.scatter_wait(l)
        update(l, items.terms, i_rows, mr * i_rows, gi, si, ip_out, ip_in, out_i, items_all)
        if l + 1 < LAYERS:
            items.gather_start(l + 1)
        users.scatter_wait(l)
        update(l, users.terms, u_rows, mc * u_rows, gu, su, up_out, up_in, out_u, users_all)
        if l + 1 < LAYERS:
            users.gather_start(l + 1)
    for l in range(LAYERS):
        items.finish(l)
        users.finish(l)


def shards(grad_users, grad_items, user_degree, item_degree, tile_values, tile_row, tile_col):
    n_row, n_col = lax.axis_size("row"), lax.axis_size("col")
    n_tiles, tile = tile_values.shape[:2]
    u_rows, width = grad_users.shape
    i_rows = grad_items.shape[0]
    u_blocks, i_blocks = u_rows * n_col // tile, i_rows * n_row // tile
    su = jnp.broadcast_to(lax.rsqrt(user_degree.astype(jnp.float32))[:, None], (u_rows, width))
    si = jnp.broadcast_to(lax.rsqrt(item_degree.astype(jnp.float32))[:, None], (i_rows, width))
    slot = jnp.arange(n_tiles, dtype=jnp.int32)

    def latest(keys, wanted, before):
        hit = (keys[None, :] == wanted[:, None]) & (slot[None, :] < before[:, None])
        return jnp.max(jnp.where(hit, slot[None, :] + 1, 0), axis=1)

    idx = jnp.concatenate(
        [
            tile_row,
            tile_col,
            latest(tile_row, tile_row, slot),
            latest(tile_col, tile_col, slot),
            latest(tile_row, jnp.arange(u_blocks, dtype=jnp.int32), jnp.full(u_blocks, n_tiles)),
            latest(tile_col, jnp.arange(i_blocks, dtype=jnp.int32), jnp.full(i_blocks, n_tiles)),
        ]
    )
    u_sub, i_sub = min(u_rows, tile), min(i_rows, tile)
    vmem = pl.BlockSpec(memory_space=pltpu.VMEM)
    bf16, f32 = jnp.bfloat16, jnp.float32
    return pl.pallas_call(
        functools.partial(kernel, n_row, n_col, n_tiles, tile, width, u_rows, i_rows),
        out_shape=(
            jax.ShapeDtypeStruct((u_rows, width), bf16),
            jax.ShapeDtypeStruct((i_rows, width), bf16),
        ),
        in_specs=[pl.BlockSpec(memory_space=pltpu.SMEM), vmem, vmem, vmem, vmem,
                  pl.BlockSpec(memory_space=pl.ANY)],
        out_specs=(vmem, vmem),
        scratch_shapes=[
            pltpu.VMEM((u_blocks, tile, width), bf16),
            pltpu.VMEM((u_blocks, tile, width), bf16),
            pltpu.VMEM((i_blocks, tile, width), bf16),
            pltpu.VMEM((i_blocks, tile, width), bf16),
            pltpu.VMEM((LAYERS, u_blocks, tile, width), bf16),
            pltpu.VMEM((LAYERS, n_col, u_rows // u_sub, u_sub, width), bf16),
            pltpu.VMEM((LAYERS, i_blocks, tile, width), bf16),
            pltpu.VMEM((LAYERS, n_row, i_rows // i_sub, i_sub, width), bf16),
            pltpu.VMEM((n_tiles + 1, tile, width), f32),
            pltpu.VMEM((n_tiles + 1, tile, width), f32),
            pltpu.VMEM((n_tiles, tile, tile), bf16),
            pltpu.VMEM((n_tiles, tile, tile), bf16),
            pltpu.SemaphoreType.DMA((LAYERS, 2, n_col)),
            pltpu.SemaphoreType.DMA((LAYERS, 2, n_col)),
            pltpu.SemaphoreType.DMA((LAYERS, 2, n_row)),
            pltpu.SemaphoreType.DMA((LAYERS, 2, n_row)),
            pltpu.SemaphoreType.DMA,
        ],
        compiler_params=pltpu.CompilerParams(
            collective_id=0, has_side_effects=True, vmem_limit_bytes=40 * 1024 * 1024
        ),
    )(idx, grad_users, grad_items, su, si, tile_values)


def solution(mesh):
    return jax.shard_map(
        shards,
        mesh=mesh,
        in_specs=(
            P(("groups", "row", "col"), None),
            P(("groups", "col", "row"), None),
            P(("groups", "row", "col")),
            P(("groups", "col", "row")),
            P(("groups", "row", "col"), None, None),
            P(("groups", "row", "col")),
            P(("groups", "row", "col")),
        ),
        out_specs=(P(("groups", "row", "col"), None), P(("groups", "col", "row"), None)),
        check_vma=False,
    )
```

```python
import functools

import jax
import jax.numpy as jnp
from jax import lax
from jax.experimental import pallas as pl
from jax.experimental.pallas import tpu as pltpu
from jax.sharding import PartitionSpec as P

LAYERS = 2
MESH = pl.DeviceIdType.MESH
WEIGHT = 1.0 / (LAYERS + 1)


def kernel(
    n_row, n_col, n_tiles, tile, width, u_rows, i_rows,
    tile_row, tile_col, gu_hbm, gi_hbm, du_hbm, di_hbm, tiles_hbm,
    out_u, out_i,
    users_0, users_1, items_0, items_1, up_out, up_in, ip_out, ip_in, sum_u, sum_i, tiles, tiles_t,
    gu, gi, du, di, su, si, prev_row, prev_col, last_row, last_col,
    u_send, u_recv, i_send, i_recv, load_sem,
):
    mr, mc = lax.axis_index("row"), lax.axis_index("col")
    u_blocks = u_rows * n_col // tile
    i_blocks = i_rows * n_row // tile

    barrier = pltpu.get_barrier_semaphore()

    def greet(axis, me, n):
        def body(d, carry):
            pl.semaphore_signal(
                barrier, inc=1, device_id={axis: lax.rem(me + d, n)}, device_id_type=MESH
            )
            return carry

        lax.fori_loop(1, n, body, 0)

    greet("row", mr, n_row)
    greet("col", mc, n_col)
    loads = [
        pltpu.make_async_copy(src, dst, load_sem.at[k])
        for k, (src, dst) in enumerate(
            ((di_hbm, di), (gi_hbm, gi), (du_hbm, du), (gu_hbm, gu), (tiles_hbm, tiles))
        )
    ]
    for load in loads:
        load.start()

    users_all, items_all = (users_0, users_1), (items_0, items_1)

    def part(ref, p, rows):
        if rows % tile == 0:
            k = rows // tile
            return ref.at[pl.ds(p * k, k)]
        per = tile // rows
        return ref.at[lax.div(p, per), pl.ds(pl.multiple_of(lax.rem(p, per) * rows, rows), rows)]

    def slot(ref, l, d, rows):
        return ref.at[l, d] if rows % tile == 0 else ref.at[l, d, 0]

    def address(at, rows, chunk):
        sub = min(rows, tile)
        return lax.div(at, sub), pl.ds(pl.multiple_of(lax.rem(at, sub), chunk), chunk)

    class Route:
        def __init__(self, axis, me, n, rows, gathered, out, inn, send, recv):
            self.n, self.rows, self.me, self.axis = n, rows, me, axis
            self.gathered, self.out, self.inn, self.send, self.recv = gathered, out, inn, send, recv
            self.relayed = n == 4
            one = me + 1 - 2 * lax.rem(me, 2)
            self.peer = (me, one, lax.rem(me + 2, 4), lax.rem(one + 2, 4))
            self.terms = 3 if self.relayed else n

        def remote(self, src, dst, l, kind, d, peer):
            return pltpu.make_async_remote_copy(
                src_ref=src,
                dst_ref=dst,
                send_sem=self.send.at[l, kind, d],
                recv_sem=self.recv.at[l, kind, d],
                device_id={self.axis: peer},
                device_id_type=MESH,
            )

        def gather(self, l, d):
            if self.relayed:
                owner, to = self.peer[2 if d == 3 else 0], self.peer[2 if d == 2 else 1]
            else:
                owner, to = self.me, lax.rem(self.me + d, self.n)
            at = part(self.gathered[l], owner, self.rows)
            return self.remote(at, at, l, 0, d, to)

        def scatter(self, l, d):
            if self.relayed:
                piece, to = self.peer[d], self.peer[2 if d == 2 else 1]
            else:
                piece = to = lax.rem(self.me + d, self.n)
            return self.remote(
                part(self.out.at[l], piece, self.rows), slot(self.inn, l, d, self.rows), l, 1, d, to
            )

        def each(self, copies, l, act, some):
            if self.relayed:
                for d in some:
                    act(copies(l, d))
            else:
                def body(d, carry):
                    act(copies(l, d))
                    return carry

                lax.fori_loop(1, self.n, body, 0)

        def gather_start(self, l):
            self.each(self.gather, l, lambda c: c.start(), (2, 1))

        def gather_relay(self, l):
            if self.relayed:
                self.gather(l, 2).wait_recv()
                self.gather(l, 3).start()

        def gather_wait(self, l):
            self.each(self.gather, l, lambda c: c.wait_recv(), (1, 3))

        def scatter_start(self, l):
            self.each(self.scatter, l, lambda c: c.start(), (3, 1))

        def scatter_relay(self, l):
            if self.relayed:
                self.scatter(l, 3).wait_recv()
                chunk = min(self.rows, 128)

                def body(k, carry):
                    at = self.peer[2] * self.rows + k * chunk
                    block = lax.div(at, tile)
                    mine = pl.ds(pl.multiple_of(lax.rem(at, tile), chunk), chunk)
                    sub, there = address(k * chunk, self.rows, chunk)
                    self.out[l, block, mine, :] = (
                        self.out[l, block, mine, :].astype(jnp.float32)
                        + self.inn[l, 3, sub, there, :].astype(jnp.float32)
                    ).astype(jnp.bfloat16)
                    return carry

                lax.fori_loop(0, self.rows // chunk, body, 0)
                self.scatter(l, 2).start()

        def scatter_wait(self, l):
            self.each(self.scatter, l, lambda c: c.wait_recv(), (1, 2))

        def finish(self, l):
            self.each(self.gather, l, lambda c: c.wait_send(), (1, 2, 3))
            self.each(self.scatter, l, lambda c: c.wait_send(), (1, 2, 3))

    items = Route("row", mr, n_row, i_rows, items_all, ip_out, ip_in, i_send, i_recv)
    users = Route("col", mc, n_col, u_rows, users_all, up_out, up_in, u_send, u_recv)

    def begin(rows, own, grad, scale, gathered):
        chunk = min(rows, 128)

        def body(k, carry):
            here = pl.ds(pl.multiple_of(k * chunk, chunk), chunk)
            now = (WEIGHT * grad[here, :].astype(jnp.float32)).astype(jnp.bfloat16)
            at = own + k * chunk
            mine = pl.ds(pl.multiple_of(lax.rem(at, tile), chunk), chunk)
            gathered[0][lax.div(at, tile), mine, :] = (
                scale[here, :] * now.astype(jnp.float32)
            ).astype(jnp.bfloat16)
            return carry

        lax.fori_loop(0, rows // chunk, body, 0)

    def scales(rows, degree, scale):
        chunk = min(rows, 128)
        for k in range(rows // chunk):
            line = lax.rsqrt(degree[k : k + 1, :].astype(jnp.float32))
            scale[k * chunk : (k + 1) * chunk, :] = jnp.broadcast_to(line, (width, chunk)).T

    loads[0].wait()
    scales(i_rows, di, si)
    loads[1].wait()
    begin(i_rows, mr * i_rows, gi, si, items_all)
    pl.semaphore_wait(barrier, n_row + n_col - 2)
    items.gather_start(0)
    loads[2].wait()
    scales(u_rows, du, su)
    loads[3].wait()
    begin(u_rows, mc * u_rows, gu, su, users_all)
    users.gather_start(0)

    def latest(keys, wanted, before):
        found = jnp.int32(0)
        for m in range(n_tiles):
            found = jnp.where((keys[m] == wanted) & (m < before), m + 1, found)
        return found

    def previous(n, carry):
        prev_row[n] = latest(tile_row, tile_row[n], n)
        prev_col[n] = latest(tile_col, tile_col[n], n)
        return carry

    def last(keys, out):
        def body(b, carry):
            out[b] = latest(keys, b, n_tiles)
            return carry

        return body

    lax.fori_loop(0, n_tiles, previous, 0)
    lax.fori_loop(0, u_blocks, last(tile_row, last_row), 0)
    lax.fori_loop(0, i_blocks, last(tile_col, last_col), 0)

    sum_u[0] = jnp.zeros((tile, width), jnp.float32)
    sum_i[0] = jnp.zeros((tile, width), jnp.float32)
    loads[4].wait()

    def turn(n, carry):
        tiles_t[n] = tiles[n].T
        return carry

    lax.fori_loop(0, n_tiles, turn, 0)

    group = 4 if n_tiles % 4 == 0 else 1

    def products(l, mats, blocks, sums, block_of, prev):
        def body(g, carry):
            parts = []
            for k in range(group):
                n = g * group + k
                b = block_of[n]
                parts.append(jnp.dot(mats[n], blocks[l][b], preferred_element_type=jnp.float32))
            for k in range(group):
                n = g * group + k
                sums[n + 1] = parts[k] + sums[prev[n]]
            return carry

        lax.fori_loop(0, n_tiles // group, body, 0)

    def stage(l, out, sums, last, blocks):
        def body(b, carry):
            out[l, b] = sums[last[b]].astype(jnp.bfloat16)
            return carry

        lax.fori_loop(0, blocks, body, 0)

    def update(l, n, rows, own, grad, scale, out, inn, result, gathered):
        chunk = min(rows, 128)

        def body(k, carry):
            here = pl.ds(pl.multiple_of(k * chunk, chunk), chunk)
            at = own + k * chunk
            block = lax.div(at, tile)
            mine = pl.ds(pl.multiple_of(lax.rem(at, tile), chunk), chunk)
            total = out[l, block, mine, :].astype(jnp.float32)
            sub, there = address(k * chunk, rows, chunk)

            def add(d, total):
                return total + inn[l, d, sub, there, :].astype(jnp.float32)

            if n <= 8:
                for d in range(1, n):
                    total = add(d, total)
            else:
                total = lax.fori_loop(1, n, add, total)
            factor = scale[here, :]
            now = (WEIGHT * grad[here, :].astype(jnp.float32) + factor * total).astype(jnp.bfloat16)
            if l + 1 < LAYERS:
                gathered[l + 1][block, mine, :] = (factor * now.astype(jnp.float32)).astype(jnp.bfloat16)
            else:
                result[here, :] = now
            return carry

        lax.fori_loop(0, rows // chunk, body, 0)

    for l in range(LAYERS):
        users.gather_relay(l)
        items.gather_relay(l)
        users.gather_wait(l)
        products(l, tiles_t, users_all, sum_i, tile_row, prev_col)
        stage(l, ip_out, sum_i, last_col, i_blocks)
        items.scatter_start(l)
        items.gather_wait(l)
        products(l, tiles, items_all, sum_u, tile_col, prev_row)
        stage(l, up_out, sum_u, last_row, u_blocks)
        users.scatter_start(l)
        items.scatter_relay(l)
        users.scatter_relay(l)
        items.scatter_wait(l)
        update(l, items.terms, i_rows, mr * i_rows, gi, si, ip_out, ip_in, out_i, items_all)
        if l + 1 < LAYERS:
            items.gather_start(l + 1)
        users.scatter_wait(l)
        update(l, users.terms, u_rows, mc * u_rows, gu, su, up_out, up_in, out_u, users_all)
        if l + 1 < LAYERS:
            users.gather_start(l + 1)
    for l in range(LAYERS):
        items.finish(l)
        users.finish(l)


def shards(grad_users, grad_items, user_degree, item_degree, tile_values, tile_row, tile_col):
    n_row, n_col = lax.axis_size("row"), lax.axis_size("col")
    n_tiles, tile = tile_values.shape[:2]
    u_rows, width = grad_users.shape
    i_rows = grad_items.shape[0]
    u_blocks, i_blocks = u_rows * n_col // tile, i_rows * n_row // tile
    u_chunk, i_chunk = min(u_rows, 128), min(i_rows, 128)
    du = user_degree.reshape(u_rows // u_chunk, u_chunk)
    di = item_degree.reshape(i_rows // i_chunk, i_chunk)
    u_sub, i_sub = min(u_rows, tile), min(i_rows, tile)
    vmem = pl.BlockSpec(memory_space=pltpu.VMEM)
    bf16, f32 = jnp.bfloat16, jnp.float32
    return pl.pallas_call(
        functools.partial(kernel, n_row, n_col, n_tiles, tile, width, u_rows, i_rows),
        out_shape=(
            jax.ShapeDtypeStruct((u_rows, width), bf16),
            jax.ShapeDtypeStruct((i_rows, width), bf16),
        ),
        in_specs=[pl.BlockSpec(memory_space=pltpu.SMEM)] * 2
        + [pl.BlockSpec(memory_space=pl.ANY)] * 5,
        out_specs=(vmem, vmem),
        scratch_shapes=[
            pltpu.VMEM((u_blocks, tile, width), bf16),
            pltpu.VMEM((u_blocks, tile, width), bf16),
            pltpu.VMEM((i_blocks, tile, width), bf16),
            pltpu.VMEM((i_blocks, tile, width), bf16),
            pltpu.VMEM((LAYERS, u_blocks, tile, width), bf16),
            pltpu.VMEM((LAYERS, n_col, u_rows // u_sub, u_sub, width), bf16),
            pltpu.VMEM((LAYERS, i_blocks, tile, width), bf16),
            pltpu.VMEM((LAYERS, n_row, i_rows // i_sub, i_sub, width), bf16),
            pltpu.VMEM((n_tiles + 1, tile, width), f32),
            pltpu.VMEM((n_tiles + 1, tile, width), f32),
            pltpu.VMEM((n_tiles, tile, tile), bf16),
            pltpu.VMEM((n_tiles, tile, tile), bf16),
            pltpu.VMEM((u_rows, width), bf16),
            pltpu.VMEM((i_rows, width), bf16),
            pltpu.VMEM(du.shape, jnp.int32),
            pltpu.VMEM(di.shape, jnp.int32),
            pltpu.VMEM((u_rows, width), f32),
            pltpu.VMEM((i_rows, width), f32),
            pltpu.SMEM((n_tiles,), jnp.int32),
            pltpu.SMEM((n_tiles,), jnp.int32),
            pltpu.SMEM((u_blocks,), jnp.int32),
            pltpu.SMEM((i_blocks,), jnp.int32),
            pltpu.SemaphoreType.DMA((LAYERS, 2, n_col)),
            pltpu.SemaphoreType.DMA((LAYERS, 2, n_col)),
            pltpu.SemaphoreType.DMA((LAYERS, 2, n_row)),
            pltpu.SemaphoreType.DMA((LAYERS, 2, n_row)),
            pltpu.SemaphoreType.DMA((5,)),
        ],
        compiler_params=pltpu.CompilerParams(
            collective_id=0, has_side_effects=True, vmem_limit_bytes=56 * 1024 * 1024
        ),
    )(tile_row, tile_col, grad_users, grad_items, du, di, tile_values)


def solution(mesh):
    return jax.shard_map(
        shards,
        mesh=mesh,
        in_specs=(
            P(("groups", "row", "col"), None),
            P(("groups", "col", "row"), None),
            P(("groups", "row", "col")),
            P(("groups", "col", "row")),
            P(("groups", "row", "col"), None, None),
            P(("groups", "row", "col")),
            P(("groups", "row", "col")),
        ),
        out_specs=(P(("groups", "row", "col"), None), P(("groups", "col", "row"), None)),
        check_vma=False,
    )
```

```python
import functools

import jax
import jax.numpy as jnp
from jax import lax
from jax.experimental import pallas as pl
from jax.experimental.pallas import tpu as pltpu
from jax.sharding import PartitionSpec as P

LAYERS = 2
MESH = pl.DeviceIdType.MESH
WEIGHT = 1.0 / (LAYERS + 1)


def kernel(
    n_row, n_col, n_tiles, tile, width, u_rows, i_rows,
    tile_row, tile_col, gu_hbm, gi_hbm, du_hbm, di_hbm, tiles_hbm,
    out_u, out_i,
    users_0, users_1, items_0, items_1, up_out, up_in, ip_out, ip_in, sum_u, sum_i, tiles, tiles_t,
    gu, gi, du, di, su, si, prev_row, prev_col, last_row, last_col,
    u_send, u_recv, i_send, i_recv, load_sem,
):
    mr, mc = lax.axis_index("row"), lax.axis_index("col")
    u_blocks = u_rows * n_col // tile
    i_blocks = i_rows * n_row // tile

    barrier = pltpu.get_barrier_semaphore()

    def greet(axis, me, n):
        def body(d, carry):
            pl.semaphore_signal(
                barrier, inc=1, device_id={axis: lax.rem(me + d, n)}, device_id_type=MESH
            )
            return carry

        lax.fori_loop(1, n, body, 0)

    greet("row", mr, n_row)
    greet("col", mc, n_col)
    loads = [
        pltpu.make_async_copy(src, dst, load_sem.at[k])
        for k, (src, dst) in enumerate(
            ((di_hbm, di), (gi_hbm, gi), (du_hbm, du), (gu_hbm, gu), (tiles_hbm, tiles))
        )
    ]
    for load in loads:
        load.start()

    users_all, items_all = (users_0, users_1), (items_0, items_1)

    def part(ref, p, rows):
        if rows % tile == 0:
            k = rows // tile
            return ref.at[pl.ds(p * k, k)]
        per = tile // rows
        return ref.at[lax.div(p, per), pl.ds(pl.multiple_of(lax.rem(p, per) * rows, rows), rows)]

    def slot(ref, l, d, rows):
        return ref.at[l, d] if rows % tile == 0 else ref.at[l, d, 0]

    def address(at, rows, chunk):
        sub = min(rows, tile)
        return lax.div(at, sub), pl.ds(pl.multiple_of(lax.rem(at, sub), chunk), chunk)

    class Route:
        def __init__(self, axis, me, n, rows, gathered, out, inn, send, recv):
            self.n, self.rows, self.me, self.axis = n, rows, me, axis
            self.gathered, self.out, self.inn, self.send, self.recv = gathered, out, inn, send, recv
            self.relayed = n == 4
            one = me + 1 - 2 * lax.rem(me, 2)
            self.peer = (me, one, lax.rem(me + 2, 4), lax.rem(one + 2, 4))
            self.terms = 3 if self.relayed else n

        def remote(self, src, dst, l, kind, d, peer):
            return pltpu.make_async_remote_copy(
                src_ref=src,
                dst_ref=dst,
                send_sem=self.send.at[l, kind, d],
                recv_sem=self.recv.at[l, kind, d],
                device_id={self.axis: peer},
                device_id_type=MESH,
            )

        def gather(self, l, d):
            if self.relayed:
                owner, to = self.peer[2 if d == 3 else 0], self.peer[2 if d == 2 else 1]
            else:
                owner, to = self.me, lax.rem(self.me + d, self.n)
            at = part(self.gathered[l], owner, self.rows)
            return self.remote(at, at, l, 0, d, to)

        def scatter(self, l, d):
            if self.relayed:
                piece, to = self.peer[d], self.peer[2 if d == 2 else 1]
            else:
                piece = to = lax.rem(self.me + d, self.n)
            return self.remote(
                part(self.out.at[l], piece, self.rows), slot(self.inn, l, d, self.rows), l, 1, d, to
            )

        def each(self, copies, l, act, some):
            if self.relayed:
                for d in some:
                    act(copies(l, d))
            else:
                def body(d, carry):
                    act(copies(l, d))
                    return carry

                lax.fori_loop(1, self.n, body, 0)

        def gather_start(self, l):
            self.each(self.gather, l, lambda c: c.start(), (2, 1))

        def gather_relay(self, l):
            if self.relayed:
                self.gather(l, 2).wait_recv()
                self.gather(l, 3).start()

        def gather_wait(self, l):
            self.each(self.gather, l, lambda c: c.wait_recv(), (1, 3))

        def scatter_start(self, l):
            self.each(self.scatter, l, lambda c: c.start(), (3,))

        def scatter_relay(self, l):
            if self.relayed:
                self.scatter(l, 3).wait_recv()
                chunk = min(self.rows, 128)

                def body(k, carry):
                    at = self.peer[2] * self.rows + k * chunk
                    block = lax.div(at, tile)
                    mine = pl.ds(pl.multiple_of(lax.rem(at, tile), chunk), chunk)
                    sub, there = address(k * chunk, self.rows, chunk)
                    self.out[l, block, mine, :] = (
                        self.out[l, block, mine, :].astype(jnp.float32)
                        + self.inn[l, 3, sub, there, :].astype(jnp.float32)
                    ).astype(jnp.bfloat16)
                    return carry

                lax.fori_loop(0, self.rows // chunk, body, 0)
                self.scatter(l, 2).start()
                self.scatter(l, 1).start()

        def scatter_wait(self, l):
            self.each(self.scatter, l, lambda c: c.wait_recv(), (1, 2))

        def finish(self, l):
            self.each(self.gather, l, lambda c: c.wait_send(), (1, 2, 3))
            self.each(self.scatter, l, lambda c: c.wait_send(), (1, 2, 3))

    items = Route("row", mr, n_row, i_rows, items_all, ip_out, ip_in, i_send, i_recv)
    users = Route("col", mc, n_col, u_rows, users_all, up_out, up_in, u_send, u_recv)

    def begin(rows, own, grad, scale, gathered):
        chunk = min(rows, 128)

        def body(k, carry):
            here = pl.ds(pl.multiple_of(k * chunk, chunk), chunk)
            now = (WEIGHT * grad[here, :].astype(jnp.float32)).astype(jnp.bfloat16)
            at = own + k * chunk
            mine = pl.ds(pl.multiple_of(lax.rem(at, tile), chunk), chunk)
            gathered[0][lax.div(at, tile), mine, :] = (
                scale[here, :] * now.astype(jnp.float32)
            ).astype(jnp.bfloat16)
            return carry

        lax.fori_loop(0, rows // chunk, body, 0)

    def scales(rows, degree, scale):
        chunk = min(rows, 128)
        for k in range(rows // chunk):
            line = lax.rsqrt(degree[k : k + 1, :].astype(jnp.float32))
            scale[k * chunk : (k + 1) * chunk, :] = jnp.broadcast_to(line, (width, chunk)).T

    loads[0].wait()
    scales(i_rows, di, si)
    loads[1].wait()
    begin(i_rows, mr * i_rows, gi, si, items_all)
    pl.semaphore_wait(barrier, n_row + n_col - 2)
    items.gather_start(0)
    loads[2].wait()
    scales(u_rows, du, su)
    loads[3].wait()
    begin(u_rows, mc * u_rows, gu, su, users_all)
    users.gather_start(0)

    def latest(keys, wanted, before):
        found = jnp.int32(0)
        for m in range(n_tiles):
            found = jnp.where((keys[m] == wanted) & (m < before), m + 1, found)
        return found

    def previous(n, carry):
        prev_row[n] = latest(tile_row, tile_row[n], n)
        prev_col[n] = latest(tile_col, tile_col[n], n)
        return carry

    def last(keys, out):
        def body(b, carry):
            out[b] = latest(keys, b, n_tiles)
            return carry

        return body


    sum_u[0] = jnp.zeros((tile, width), jnp.float32)
    sum_i[0] = jnp.zeros((tile, width), jnp.float32)

    def turn(n, carry):
        tiles_t[n] = tiles[n].T
        return carry


    group = 4 if n_tiles % 4 == 0 else 1

    def products(l, mats, blocks, sums, block_of, prev):
        def body(g, carry):
            parts = []
            for k in range(group):
                n = g * group + k
                b = block_of[n]
                parts.append(jnp.dot(mats[n], blocks[l][b], preferred_element_type=jnp.float32))
            for k in range(group):
                n = g * group + k
                sums[n + 1] = parts[k] + sums[prev[n]]
            return carry

        lax.fori_loop(0, n_tiles // group, body, 0)

    def stage(l, out, sums, last, blocks):
        def body(b, carry):
            out[l, b] = sums[last[b]].astype(jnp.bfloat16)
            return carry

        lax.fori_loop(0, blocks, body, 0)

    def update(l, n, rows, own, grad, scale, out, inn, result, gathered):
        chunk = min(rows, 128)

        def body(k, carry):
            here = pl.ds(pl.multiple_of(k * chunk, chunk), chunk)
            at = own + k * chunk
            block = lax.div(at, tile)
            mine = pl.ds(pl.multiple_of(lax.rem(at, tile), chunk), chunk)
            total = out[l, block, mine, :].astype(jnp.float32)
            sub, there = address(k * chunk, rows, chunk)

            def add(d, total):
                return total + inn[l, d, sub, there, :].astype(jnp.float32)

            if n <= 8:
                for d in range(1, n):
                    total = add(d, total)
            else:
                total = lax.fori_loop(1, n, add, total)
            factor = scale[here, :]
            now = (WEIGHT * grad[here, :].astype(jnp.float32) + factor * total).astype(jnp.bfloat16)
            if l + 1 < LAYERS:
                gathered[l + 1][block, mine, :] = (factor * now.astype(jnp.float32)).astype(jnp.bfloat16)
            else:
                result[here, :] = now
            return carry

        lax.fori_loop(0, rows // chunk, body, 0)

    for l in range(LAYERS):
        users.gather_relay(l)
        items.gather_relay(l)
        if l == 0:
            loads[4].wait()
            lax.fori_loop(0, n_tiles, previous, 0)
            lax.fori_loop(0, u_blocks, last(tile_row, last_row), 0)
            lax.fori_loop(0, i_blocks, last(tile_col, last_col), 0)
            lax.fori_loop(0, n_tiles, turn, 0)
        users.gather_wait(l)
        products(l, tiles_t, users_all, sum_i, tile_row, prev_col)
        stage(l, ip_out, sum_i, last_col, i_blocks)
        items.scatter_start(l)
        items.gather_wait(l)
        products(l, tiles, items_all, sum_u, tile_col, prev_row)
        stage(l, up_out, sum_u, last_row, u_blocks)
        users.scatter_start(l)
        items.scatter_relay(l)
        users.scatter_relay(l)
        items.scatter_wait(l)
        update(l, items.terms, i_rows, mr * i_rows, gi, si, ip_out, ip_in, out_i, items_all)
        if l + 1 < LAYERS:
            items.gather_start(l + 1)
        users.scatter_wait(l)
        update(l, users.terms, u_rows, mc * u_rows, gu, su, up_out, up_in, out_u, users_all)
        if l + 1 < LAYERS:
            users.gather_start(l + 1)
    for l in range(LAYERS):
        items.finish(l)
        users.finish(l)


def shards(grad_users, grad_items, user_degree, item_degree, tile_values, tile_row, tile_col):
    n_row, n_col = lax.axis_size("row"), lax.axis_size("col")
    n_tiles, tile = tile_values.shape[:2]
    u_rows, width = grad_users.shape
    i_rows = grad_items.shape[0]
    u_blocks, i_blocks = u_rows * n_col // tile, i_rows * n_row // tile
    u_chunk, i_chunk = min(u_rows, 128), min(i_rows, 128)
    du = user_degree.reshape(u_rows // u_chunk, u_chunk)
    di = item_degree.reshape(i_rows // i_chunk, i_chunk)
    u_sub, i_sub = min(u_rows, tile), min(i_rows, tile)
    vmem = pl.BlockSpec(memory_space=pltpu.VMEM)
    bf16, f32 = jnp.bfloat16, jnp.float32
    return pl.pallas_call(
        functools.partial(kernel, n_row, n_col, n_tiles, tile, width, u_rows, i_rows),
        out_shape=(
            jax.ShapeDtypeStruct((u_rows, width), bf16),
            jax.ShapeDtypeStruct((i_rows, width), bf16),
        ),
        in_specs=[pl.BlockSpec(memory_space=pltpu.SMEM)] * 2
        + [pl.BlockSpec(memory_space=pl.ANY)] * 5,
        out_specs=(vmem, vmem),
        scratch_shapes=[
            pltpu.VMEM((u_blocks, tile, width), bf16),
            pltpu.VMEM((u_blocks, tile, width), bf16),
            pltpu.VMEM((i_blocks, tile, width), bf16),
            pltpu.VMEM((i_blocks, tile, width), bf16),
            pltpu.VMEM((LAYERS, u_blocks, tile, width), bf16),
            pltpu.VMEM((LAYERS, n_col, u_rows // u_sub, u_sub, width), bf16),
            pltpu.VMEM((LAYERS, i_blocks, tile, width), bf16),
            pltpu.VMEM((LAYERS, n_row, i_rows // i_sub, i_sub, width), bf16),
            pltpu.VMEM((n_tiles + 1, tile, width), f32),
            pltpu.VMEM((n_tiles + 1, tile, width), f32),
            pltpu.VMEM((n_tiles, tile, tile), bf16),
            pltpu.VMEM((n_tiles, tile, tile), bf16),
            pltpu.VMEM((u_rows, width), bf16),
            pltpu.VMEM((i_rows, width), bf16),
            pltpu.VMEM(du.shape, jnp.int32),
            pltpu.VMEM(di.shape, jnp.int32),
            pltpu.VMEM((u_rows, width), f32),
            pltpu.VMEM((i_rows, width), f32),
            pltpu.SMEM((n_tiles,), jnp.int32),
            pltpu.SMEM((n_tiles,), jnp.int32),
            pltpu.SMEM((u_blocks,), jnp.int32),
            pltpu.SMEM((i_blocks,), jnp.int32),
            pltpu.SemaphoreType.DMA((LAYERS, 2, n_col)),
            pltpu.SemaphoreType.DMA((LAYERS, 2, n_col)),
            pltpu.SemaphoreType.DMA((LAYERS, 2, n_row)),
            pltpu.SemaphoreType.DMA((LAYERS, 2, n_row)),
            pltpu.SemaphoreType.DMA((5,)),
        ],
        compiler_params=pltpu.CompilerParams(
            collective_id=0, has_side_effects=True, vmem_limit_bytes=56 * 1024 * 1024
        ),
    )(tile_row, tile_col, grad_users, grad_items, du, di, tile_values)


def solution(mesh):
    return jax.shard_map(
        shards,
        mesh=mesh,
        in_specs=(
            P(("groups", "row", "col"), None),
            P(("groups", "col", "row"), None),
            P(("groups", "row", "col")),
            P(("groups", "col", "row")),
            P(("groups", "row", "col"), None, None),
            P(("groups", "row", "col")),
            P(("groups", "row", "col")),
        ),
        out_specs=(P(("groups", "row", "col"), None), P(("groups", "col", "row"), None)),
        check_vma=False,
    )
```

```python
import functools

import jax
import jax.numpy as jnp
from jax import lax
from jax.experimental import pallas as pl
from jax.experimental.pallas import tpu as pltpu
from jax.sharding import PartitionSpec as P

LAYERS = 2
MESH = pl.DeviceIdType.MESH
WEIGHT = 1.0 / (LAYERS + 1)


def kernel(
    n_row, n_col, n_tiles, tile, width, u_rows, i_rows,
    tile_row, tile_col, gu_hbm, gi_hbm, du_hbm, di_hbm, tiles_hbm,
    out_u, out_i,
    users_0, users_1, items_0, items_1, up_out, up_in, ip_out, ip_in, sum_u, sum_i, tiles, tiles_t,
    gu, gi, du, di, su, si, prev_row, prev_col, last_row, last_col,
    u_send, u_recv, i_send, i_recv, load_sem,
):
    mr, mc = lax.axis_index("row"), lax.axis_index("col")
    u_blocks = u_rows * n_col // tile
    i_blocks = i_rows * n_row // tile

    barrier = pltpu.get_barrier_semaphore()

    def greet(axis, me, n):
        def body(d, carry):
            pl.semaphore_signal(
                barrier, inc=1, device_id={axis: lax.rem(me + d, n)}, device_id_type=MESH
            )
            return carry

        lax.fori_loop(1, n, body, 0)

    greet("row", mr, n_row)
    greet("col", mc, n_col)
    loads = [
        pltpu.make_async_copy(src, dst, load_sem.at[k])
        for k, (src, dst) in enumerate(
            ((di_hbm, di), (gi_hbm, gi), (du_hbm, du), (gu_hbm, gu), (tiles_hbm, tiles))
        )
    ]
    for load in loads:
        load.start()

    users_all, items_all = (users_0, users_1), (items_0, items_1)

    def part(ref, p, rows):
        if rows % tile == 0:
            k = rows // tile
            return ref.at[pl.ds(p * k, k)]
        per = tile // rows
        return ref.at[lax.div(p, per), pl.ds(pl.multiple_of(lax.rem(p, per) * rows, rows), rows)]

    def slot(ref, l, d, rows):
        return ref.at[l, d] if rows % tile == 0 else ref.at[l, d, 0]

    def address(at, rows, chunk):
        sub = min(rows, tile)
        return lax.div(at, sub), pl.ds(pl.multiple_of(lax.rem(at, sub), chunk), chunk)

    class Route:
        def __init__(self, axis, me, n, rows, gathered, out, inn, send, recv):
            self.n, self.rows, self.me, self.axis = n, rows, me, axis
            self.gathered, self.out, self.inn, self.send, self.recv = gathered, out, inn, send, recv
            self.relayed = n == 4
            self.halves = 2 if self.relayed and rows % (2 * tile) == 0 else 1
            one = me + 1 - 2 * lax.rem(me, 2)
            self.peer = (me, one, lax.rem(me + 2, 4), lax.rem(one + 2, 4))
            self.terms = 3 if self.relayed else n

        def remote(self, src, dst, l, kind, d, h, peer):
            if self.halves > 1:
                k = self.rows // tile // self.halves
                src, dst = src.at[pl.ds(h * k, k)], dst.at[pl.ds(h * k, k)]
            d = h * self.n + d
            return pltpu.make_async_remote_copy(
                src_ref=src,
                dst_ref=dst,
                send_sem=self.send.at[l, kind, d],
                recv_sem=self.recv.at[l, kind, d],
                device_id={self.axis: peer},
                device_id_type=MESH,
            )

        def gather(self, l, d, h=0):
            if self.relayed:
                owner, to = self.peer[2 if d == 3 else 0], self.peer[2 if d == 2 else 1]
            else:
                owner, to = self.me, lax.rem(self.me + d, self.n)
            at = part(self.gathered[l], owner, self.rows)
            return self.remote(at, at, l, 0, d, h, to)

        def scatter(self, l, d, h=0):
            if self.relayed:
                piece, to = self.peer[d], self.peer[2 if d == 2 else 1]
            else:
                piece = to = lax.rem(self.me + d, self.n)
            return self.remote(
                part(self.out.at[l], piece, self.rows), slot(self.inn, l, d, self.rows), l, 1, d, h, to
            )

        def each(self, copies, l, act, some):
            if self.relayed:
                for d in some:
                    for h in range(self.halves):
                        act(copies(l, d, h))
            else:
                def body(d, carry):
                    act(copies(l, d))
                    return carry

                lax.fori_loop(1, self.n, body, 0)

        def gather_start(self, l):
            self.each(self.gather, l, lambda c: c.start(), (2, 1))

        def gather_relay(self, l):
            if self.relayed:
                for h in range(self.halves):
                    self.gather(l, 2, h).wait_recv()
                    self.gather(l, 3, h).start()

        def gather_wait(self, l):
            self.each(self.gather, l, lambda c: c.wait_recv(), (1, 3))

        def scatter_start(self, l):
            self.each(self.scatter, l, lambda c: c.start(), (3,))

        def scatter_relay(self, l):
            if self.relayed:
                chunk = min(self.rows, 128)

                def body(k, carry):
                    at = self.peer[2] * self.rows + k * chunk
                    block = lax.div(at, tile)
                    mine = pl.ds(pl.multiple_of(lax.rem(at, tile), chunk), chunk)
                    sub, there = address(k * chunk, self.rows, chunk)
                    self.out[l, block, mine, :] = (
                        self.out[l, block, mine, :].astype(jnp.float32)
                        + self.inn[l, 3, sub, there, :].astype(jnp.float32)
                    ).astype(jnp.bfloat16)
                    return carry

                count = self.rows // chunk // self.halves
                for h in range(self.halves):
                    self.scatter(l, 3, h).wait_recv()
                    lax.fori_loop(h * count, (h + 1) * count, body, 0)
                    self.scatter(l, 2, h).start()
                for h in range(self.halves):
                    self.scatter(l, 1, h).start()

        def scatter_wait(self, l):
            self.each(self.scatter, l, lambda c: c.wait_recv(), (1, 2))

        def finish(self, l):
            self.each(self.gather, l, lambda c: c.wait_send(), (1, 2, 3))
            self.each(self.scatter, l, lambda c: c.wait_send(), (1, 2, 3))

    items = Route("row", mr, n_row, i_rows, items_all, ip_out, ip_in, i_send, i_recv)
    users = Route("col", mc, n_col, u_rows, users_all, up_out, up_in, u_send, u_recv)

    def begin(rows, own, grad, scale, gathered):
        chunk = min(rows, 128)

        def body(k, carry):
            here = pl.ds(pl.multiple_of(k * chunk, chunk), chunk)
            now = (WEIGHT * grad[here, :].astype(jnp.float32)).astype(jnp.bfloat16)
            at = own + k * chunk
            mine = pl.ds(pl.multiple_of(lax.rem(at, tile), chunk), chunk)
            gathered[0][lax.div(at, tile), mine, :] = (
                scale[here, :] * now.astype(jnp.float32)
            ).astype(jnp.bfloat16)
            return carry

        lax.fori_loop(0, rows // chunk, body, 0)

    def scales(rows, degree, scale):
        chunk = min(rows, 128)
        for k in range(rows // chunk):
            line = lax.rsqrt(degree[k : k + 1, :].astype(jnp.float32))
            scale[k * chunk : (k + 1) * chunk, :] = jnp.broadcast_to(line, (width, chunk)).T

    loads[0].wait()
    scales(i_rows, di, si)
    loads[1].wait()
    begin(i_rows, mr * i_rows, gi, si, items_all)
    pl.semaphore_wait(barrier, n_row + n_col - 2)
    items.gather_start(0)
    loads[2].wait()
    scales(u_rows, du, su)
    loads[3].wait()
    begin(u_rows, mc * u_rows, gu, su, users_all)
    users.gather_start(0)

    def latest(keys, wanted, before):
        found = jnp.int32(0)
        for m in range(n_tiles):
            found = jnp.where((keys[m] == wanted) & (m < before), m + 1, found)
        return found

    def previous(n, carry):
        prev_row[n] = latest(tile_row, tile_row[n], n)
        prev_col[n] = latest(tile_col, tile_col[n], n)
        return carry

    def last(keys, out):
        def body(b, carry):
            out[b] = latest(keys, b, n_tiles)
            return carry

        return body


    sum_u[0] = jnp.zeros((tile, width), jnp.float32)
    sum_i[0] = jnp.zeros((tile, width), jnp.float32)

    def turn(n, carry):
        tiles_t[n] = tiles[n].T
        return carry


    group = 8 if n_tiles % 8 == 0 else 1

    def products(l, mats, blocks, sums, block_of, prev):
        def body(g, carry):
            parts = []
            for k in range(group):
                n = g * group + k
                b = block_of[n]
                parts.append(jnp.dot(mats[n], blocks[l][b], preferred_element_type=jnp.float32))
            for k in range(group):
                n = g * group + k
                sums[n + 1] = parts[k] + sums[prev[n]]
            return carry

        lax.fori_loop(0, n_tiles // group, body, 0)

    def stage(l, out, sums, last, blocks):
        def body(b, carry):
            out[l, b] = sums[last[b]].astype(jnp.bfloat16)
            return carry

        lax.fori_loop(0, blocks, body, 0)

    def update(l, n, rows, own, grad, scale, out, inn, result, gathered):
        chunk = min(rows, 128)

        def body(k, carry):
            here = pl.ds(pl.multiple_of(k * chunk, chunk), chunk)
            at = own + k * chunk
            block = lax.div(at, tile)
            mine = pl.ds(pl.multiple_of(lax.rem(at, tile), chunk), chunk)
            total = out[l, block, mine, :].astype(jnp.float32)
            sub, there = address(k * chunk, rows, chunk)

            def add(d, total):
                return total + inn[l, d, sub, there, :].astype(jnp.float32)

            if n <= 8:
                for d in range(1, n):
                    total = add(d, total)
            else:
                total = lax.fori_loop(1, n, add, total)
            factor = scale[here, :]
            now = (WEIGHT * grad[here, :].astype(jnp.float32) + factor * total).astype(jnp.bfloat16)
            if l + 1 < LAYERS:
                gathered[l + 1][block, mine, :] = (factor * now.astype(jnp.float32)).astype(jnp.bfloat16)
            else:
                result[here, :] = now
            return carry

        lax.fori_loop(0, rows // chunk, body, 0)

    for l in range(LAYERS):
        users.gather_relay(l)
        items.gather_relay(l)
        if l == 0:
            loads[4].wait()
            lax.fori_loop(0, n_tiles, previous, 0)
            lax.fori_loop(0, u_blocks, last(tile_row, last_row), 0)
            lax.fori_loop(0, i_blocks, last(tile_col, last_col), 0)
            lax.fori_loop(0, n_tiles, turn, 0)
        users.gather_wait(l)
        products(l, tiles_t, users_all, sum_i, tile_row, prev_col)
        stage(l, ip_out, sum_i, last_col, i_blocks)
        items.scatter_start(l)
        items.gather_wait(l)
        products(l, tiles, items_all, sum_u, tile_col, prev_row)
        stage(l, up_out, sum_u, last_row, u_blocks)
        users.scatter_start(l)
        items.scatter_relay(l)
        users.scatter_relay(l)
        items.scatter_wait(l)
        update(l, items.terms, i_rows, mr * i_rows, gi, si, ip_out, ip_in, out_i, items_all)
        if l + 1 < LAYERS:
            items.gather_start(l + 1)
        users.scatter_wait(l)
        update(l, users.terms, u_rows, mc * u_rows, gu, su, up_out, up_in, out_u, users_all)
        if l + 1 < LAYERS:
            users.gather_start(l + 1)
    for l in range(LAYERS):
        items.finish(l)
        users.finish(l)


def shards(grad_users, grad_items, user_degree, item_degree, tile_values, tile_row, tile_col):
    n_row, n_col = lax.axis_size("row"), lax.axis_size("col")
    n_tiles, tile = tile_values.shape[:2]
    u_rows, width = grad_users.shape
    i_rows = grad_items.shape[0]
    u_blocks, i_blocks = u_rows * n_col // tile, i_rows * n_row // tile
    u_chunk, i_chunk = min(u_rows, 128), min(i_rows, 128)
    du = user_degree.reshape(u_rows // u_chunk, u_chunk)
    di = item_degree.reshape(i_rows // i_chunk, i_chunk)
    u_sub, i_sub = min(u_rows, tile), min(i_rows, tile)
    vmem = pl.BlockSpec(memory_space=pltpu.VMEM)
    bf16, f32 = jnp.bfloat16, jnp.float32
    return pl.pallas_call(
        functools.partial(kernel, n_row, n_col, n_tiles, tile, width, u_rows, i_rows),
        out_shape=(
            jax.ShapeDtypeStruct((u_rows, width), bf16),
            jax.ShapeDtypeStruct((i_rows, width), bf16),
        ),
        in_specs=[pl.BlockSpec(memory_space=pltpu.SMEM)] * 2
        + [pl.BlockSpec(memory_space=pl.ANY)] * 5,
        out_specs=(vmem, vmem),
        scratch_shapes=[
            pltpu.VMEM((u_blocks, tile, width), bf16),
            pltpu.VMEM((u_blocks, tile, width), bf16),
            pltpu.VMEM((i_blocks, tile, width), bf16),
            pltpu.VMEM((i_blocks, tile, width), bf16),
            pltpu.VMEM((LAYERS, u_blocks, tile, width), bf16),
            pltpu.VMEM((LAYERS, n_col, u_rows // u_sub, u_sub, width), bf16),
            pltpu.VMEM((LAYERS, i_blocks, tile, width), bf16),
            pltpu.VMEM((LAYERS, n_row, i_rows // i_sub, i_sub, width), bf16),
            pltpu.VMEM((n_tiles + 1, tile, width), f32),
            pltpu.VMEM((n_tiles + 1, tile, width), f32),
            pltpu.VMEM((n_tiles, tile, tile), bf16),
            pltpu.VMEM((n_tiles, tile, tile), bf16),
            pltpu.VMEM((u_rows, width), bf16),
            pltpu.VMEM((i_rows, width), bf16),
            pltpu.VMEM(du.shape, jnp.int32),
            pltpu.VMEM(di.shape, jnp.int32),
            pltpu.VMEM((u_rows, width), f32),
            pltpu.VMEM((i_rows, width), f32),
            pltpu.SMEM((n_tiles,), jnp.int32),
            pltpu.SMEM((n_tiles,), jnp.int32),
            pltpu.SMEM((u_blocks,), jnp.int32),
            pltpu.SMEM((i_blocks,), jnp.int32),
            pltpu.SemaphoreType.DMA((LAYERS, 2, 2 * n_col)),
            pltpu.SemaphoreType.DMA((LAYERS, 2, 2 * n_col)),
            pltpu.SemaphoreType.DMA((LAYERS, 2, 2 * n_row)),
            pltpu.SemaphoreType.DMA((LAYERS, 2, 2 * n_row)),
            pltpu.SemaphoreType.DMA((5,)),
        ],
        compiler_params=pltpu.CompilerParams(
            collective_id=0, has_side_effects=True, vmem_limit_bytes=56 * 1024 * 1024
        ),
    )(tile_row, tile_col, grad_users, grad_items, du, di, tile_values)


def solution(mesh):
    return jax.shard_map(
        shards,
        mesh=mesh,
        in_specs=(
            P(("groups", "row", "col"), None),
            P(("groups", "col", "row"), None),
            P(("groups", "row", "col")),
            P(("groups", "col", "row")),
            P(("groups", "row", "col"), None, None),
            P(("groups", "row", "col")),
            P(("groups", "row", "col")),
        ),
        out_specs=(P(("groups", "row", "col"), None), P(("groups", "col", "row"), None)),
        check_vma=False,
    )
```
